32 devices in a mesh: groups: 1, expert: 32 (over z, y, x, core).
Axes of the slice: x: 2, y: 2, z: 4, core: 2. Of those that a mesh axis runs over, the one named last changes fastest.
Arguments:
- attn_heads: bfloat16 [32, 256, 256], P(('groups', 'expert')), may hold values from -6 to 6
- out_proj: bfloat16 [32, 256, 4096], P('expert'), may hold values from -0.09375 to 0.09375
- norm_gain: bfloat16 [4096], replicated, may hold values from 0.099609375 to 1.8984375
- routes: int32 [512, 8], P(('groups', 'expert')), may hold values from 0 to 15, all different within a row; in each aligned block of 16 rows (0 to 15, 16 to 31, ...) at most 16 rows name the same one
- gate_weights: float32 [512, 8], P(('groups', 'expert')), may hold values from 0.05 to 0.4
- expert_home: int32 [16], replicated, may hold values from 0 to 15, each once
- w_gate: bfloat16 [32, 4096, 384], P('expert'), may hold values from -0.09375 to 0.09375
- w_up: bfloat16 [32, 4096, 384], P('expert'), may hold values from -0.09375 to 0.09375
- w_down: bfloat16 [32, 384, 4096], P('expert'), may hold values from -0.21875 to 0.21875
Outputs:
- block_out: bfloat16 [512, 4096], P(('groups', 'expert'))
The draws below stay inside these ranges and needn't reach their ends.
Inputs may be any that keep to these rules, and one draw needn't show every extreme that they name: `routes`: in each block of 16 rows (one device's tokens) no expert is named more than 16 times, a bound that some block reaches; a row names 8 different experts. `expert_home`: A permutation: each pair of devices holds exactly one expert.
All inputs are finite; a program needn't handle non-finite values.
Results may differ from the reference program's by a relative error of at most 0.014.
Values may be sent and summed in bfloat16 or wider, within the bound.
A program may use at most 128 MiB of HBM per device.

```python
import math
import jax
import jax.numpy as jnp
import numpy as np
from jax import lax

D = 4096
HEADS = 32
HD = 128
TP = 16
FF = 768
TOP = 8
TOK_DEV = 16
HEADS_DEV = 2
FFH = 384
EXPERTS = 16
TG = 256
TOKENS = 512
CAP = 16
N_EXPERT = 32


def block_levels(rng, dims, pieces, low, largest):
    gain = 1.0
    for position, parts in pieces:
        draws = jax.random.uniform(jax.random.fold_in(jax.random.fold_in(rng, 6), position), (parts,), jnp.float32, low / len(pieces), largest / len(pieces))
        gain = gain * jnp.repeat(jnp.exp(draws), dims[position] // parts).reshape((-1,) + (1,) * (len(dims) - 1 - position))
    return gain


def deal_out(rng, own, number, rows, count, top, limit, skew):
    sequence = jax.random.permutation(rng, count)
    crowded, usual = portions_of(count, rows * top, limit, skew, True), portions_of(count, rows * top, limit, skew, False)
    places = jnp.arange(count)

    def named(lengths, turn):
        used = int((lengths > 0).sum())
        fixed = max(1, used // 4)
        moved = fixed + (places - fixed + turn * (used - fixed)) % max(1, count - fixed)
        return jnp.zeros((count,), jnp.int32).at[sequence[jnp.where(places < fixed, places, moved)]].set(jnp.asarray(lengths, jnp.int32))

    lengths = jnp.where(number % 4 == 0, named(crowded, number // 4), named(usual, number - number // 4 - 1))
    mixed = jax.random.permutation(jax.random.fold_in(own, 3), count)
    giver, receiver = mixed[0:count // 2 * 2:2], mixed[1:count // 2 * 2:2]
    room = jnp.minimum(lengths[giver] - 1, limit - lengths[receiver]) // 2
    room = jnp.where((giver == sequence[0]) | (receiver == sequence[0]) | (lengths[receiver] == 0), 0, jnp.maximum(room, 0))
    moved = jax.random.randint(jax.random.fold_in(own, 4), (count // 2,), 0, 1 << 20) % (room + 1)
    lengths = lengths.at[giver].add(-moved).at[receiver].add(moved)
    labels = jnp.searchsorted(jnp.cumsum(lengths), jnp.arange(rows * top), side="right").astype(jnp.int32)
    table = labels.reshape(top, rows).T
    table = table[jax.random.permutation(jax.random.fold_in(own, 1), rows)]
    turn = jax.random.randint(jax.random.fold_in(own, 2), (rows, 1), 0, top)
    return jnp.take_along_axis(table, (jnp.arange(top)[None, :] + turn) % top, axis=1)


def portions_of(amount, total, bound, slope, full):
    loads = [(1 << 20) // math.isqrt(standing ** slope) + 1 for standing in range(1, amount + 1)]
    largest = bound if full else min(bound, max(-(-total // amount), total * loads[0] // sum(loads)))
    least = 1 if total - largest >= amount - 1 else 0
    given, spare = [largest] + [least] * (amount - 1), total - largest - least * (amount - 1)
    while spare > 0:
        free = [i for i in range(1, amount) if given[i] < largest] or [i for i in range(1, amount) if given[i] < bound]
        whole, remaining = sum([loads[i] for i in free]), spare
        for i in free:
            more = min(bound - given[i], max(1, remaining * loads[i] // whole), spare)
            given[i] = given[i] + more
            spare = spare - more
    return np.array(given)


def normal_values(stream_key, dims, deviation, reach, split=(), kind=jnp.bfloat16):
    level = block_levels(stream_key, dims, split, -0.22, 0.18) if split else 1.0
    values = jax.random.normal(stream_key, dims, jnp.float32) * deviation * level
    return jnp.minimum(jnp.maximum(values, -reach), reach).astype(kind)


def setup_inputs(seed: int = 0, part: int = 0) -> dict:
    splits = jax.random.split(jax.random.key(seed), 10)
    part_keys = jax.random.split(jax.random.fold_in(splits[9], part), 10)
    attn_heads = normal_values(part_keys[0], (N_EXPERT, TG, HEADS_DEV * HD), 1.0, 6.0, ((0, 32),))
    out_proj = normal_values(splits[1], (N_EXPERT, HEADS_DEV * HD, D), (HEADS * HD) ** -0.5, 0.09375, ((0, 32),))
    norm_gain = jnp.clip(1.0 + 0.18 * jax.random.normal(splits[2], (D,), jnp.float32), 0.099609375, 1.8984375).astype(jnp.bfloat16)
    routes_keys = jax.random.split(jax.random.fold_in(part_keys[3], 1), TOKENS // TOK_DEV)
    routes_turns = jax.random.permutation(jax.random.fold_in(part_keys[3], 3), TOKENS // TOK_DEV)
    routes = jax.vmap(lambda own, number: deal_out(jax.random.fold_in(part_keys[3], 2), own, number, TOK_DEV, EXPERTS, TOP, CAP, 2))(routes_keys, routes_turns).reshape((TOKENS, TOP))
    gate_weights = jnp.clip(jnp.exp(math.log(0.4) - 2.0794415 * jax.random.uniform(part_keys[4], (TOKENS, TOP), jnp.float32) ** block_levels(part_keys[4], (TOKENS, TOP), ((0, 32),), -0.2, 0.2)), 0.05, 0.4)
    expert_home = jax.random.permutation(splits[5], EXPERTS).astype(jnp.int32)
    w_gate = normal_values(splits[6], (N_EXPERT, D, FFH), D ** -0.5, 0.09375, ((0, 32),))
    w_up = normal_values(splits[7], (N_EXPERT, D, FFH), D ** -0.5, 0.09375, ((0, 32),))
    w_down = normal_values(splits[8], (N_EXPERT, FFH, D), FF ** -0.5, 0.21875, ((0, 32),))
    return {"attn_heads": attn_heads, "out_proj": out_proj, "norm_gain": norm_gain, "routes": routes, "gate_weights": gate_weights, "expert_home": expert_home, "w_gate": w_gate, "w_up": w_up, "w_down": w_down}


def reference(attn_heads, out_proj, norm_gain, routes, gate_weights, expert_home, w_gate, w_up, w_down):
    groups = N_EXPERT // TP
    columns = HEADS_DEV * HD

    def project(pair_in):
        heads_in, weights_in = pair_in
        part = jnp.einsum('htc,hcd->htd', heads_in.astype(jnp.float32), weights_in.astype(jnp.float32))
        part = part.astype(jnp.bfloat16)
        return lax.optimization_barrier(jnp.sum(part.astype(jnp.float32), axis=0))
    state = lax.map(project, (attn_heads.reshape(groups, TP, TG, columns), out_proj.reshape(groups, TP, columns, D)))
    state = state.reshape(TOKENS, D)
    scale = lax.rsqrt(lax.optimization_barrier(jnp.mean(state * state, axis=-1, keepdims=True)) + 1e-06)
    normed = (state * scale * norm_gain.astype(jnp.float32)).astype(jnp.bfloat16)
    flat = routes.reshape(N_EXPERT, TOK_DEV * TOP).astype(jnp.int32)
    choose = (flat[:, :, None] == jnp.arange(EXPERTS, dtype=jnp.int32)[None, None, :]).astype(jnp.int32)
    earlier = jnp.cumsum(choose, axis=1) - choose
    slot = lax.optimization_barrier(jnp.sum(earlier * choose, axis=2)).astype(jnp.int32)
    source = jnp.arange(N_EXPERT, dtype=jnp.int32)[:, None]
    column = (source * CAP + slot).astype(jnp.int32)
    token_index = (jnp.arange(TOKENS * TOP, dtype=jnp.int32) // TOP).reshape(N_EXPERT, TOK_DEV * TOP)
    buffer = jnp.zeros((EXPERTS, N_EXPERT * CAP, D), jnp.bfloat16).at[flat, column].set(normed[token_index])
    gate_all = w_gate.reshape(EXPERTS, 2, D, FFH)
    up_all = w_up.reshape(EXPERTS, 2, D, FFH)
    down_all = w_down.reshape(EXPERTS, 2 * FFH, D)

    def expert_ffn(item):
        rows_in, home = item
        w_one = lax.dynamic_index_in_dim(gate_all, home, 0, keepdims=False)
        w_one = jnp.transpose(w_one, (1, 0, 2)).reshape(D, FF)
        w_three = lax.dynamic_index_in_dim(up_all, home, 0, keepdims=False)
        w_three = jnp.transpose(w_three, (1, 0, 2)).reshape(D, FF)
        w_two = lax.dynamic_index_in_dim(down_all, home, 0, keepdims=False)
        gate = jnp.dot(rows_in, w_one, preferred_element_type=jnp.float32)
        upper = jnp.dot(rows_in, w_three, preferred_element_type=jnp.float32)
        act = (jax.nn.silu(gate) * upper).astype(jnp.bfloat16)
        return jnp.dot(act, w_two, preferred_element_type=jnp.float32).astype(jnp.bfloat16)
    outputs = lax.map(expert_ffn, (buffer, expert_home.astype(jnp.int32)))
    picked = outputs[flat, column].astype(jnp.float32).reshape(TOKENS, TOP, D)
    mixture = lax.optimization_barrier(jnp.sum(picked * gate_weights.astype(jnp.float32)[:, :, None], axis=1))
    return (state + mixture).astype(jnp.bfloat16)
```

```python
import jax
import jax.numpy as jnp
from jax import lax
from jax.sharding import PartitionSpec as P

TP = 16


def body(attn_heads, out_proj, norm_gain, routes, gate_weights, expert_home, w_gate, w_up, w_down):
    devices = lax.axis_size("expert")
    here = lax.axis_index("expert")
    experts_all = expert_home.shape[0]
    groups = [list(range(g * TP, (g + 1) * TP)) for g in range(devices // TP)]
    partial_value = jnp.dot(attn_heads[0], out_proj[0], preferred_element_type=jnp.float32).astype(
        jnp.bfloat16
    )
    state = lax.psum_scatter(
        partial_value, "expert", scatter_dimension=0, axis_index_groups=groups, tiled=True
    ).astype(jnp.float32)
    scale = lax.rsqrt(jnp.mean(state * state, axis=-1, keepdims=True) + 1e-06)
    normed = (state * scale * norm_gain.astype(jnp.float32)).astype(jnp.bfloat16)
    mine = routes[:, :, None] == jnp.arange(experts_all, dtype=jnp.int32)
    dense = jnp.sum(jnp.where(mine, gate_weights[:, :, None], 0.0), axis=1)
    dense = lax.all_gather(dense, "expert", axis=0, tiled=True)
    gate_here = jnp.sum(jnp.where(expert_home[None, :] == here // 2, dense, 0.0), axis=1, keepdims=True)
    rows = lax.all_gather(normed, "expert", axis=0, tiled=True)
    gate = jnp.dot(rows, w_gate[0], preferred_element_type=jnp.float32)
    upper = jnp.dot(rows, w_up[0], preferred_element_type=jnp.float32)
    act = (jax.nn.silu(gate) * upper).astype(jnp.bfloat16)
    part = jnp.dot(act, w_down[0], preferred_element_type=jnp.float32) * gate_here
    mixture = lax.psum_scatter(
        part.astype(jnp.bfloat16), "expert", scatter_dimension=0, tiled=True
    ).astype(jnp.float32)
    return (state + mixture).astype(jnp.bfloat16)


def solution(mesh):
    placed = (
        P(("groups", "expert"), None, None),
        P("expert", None, None),
        P(),
        P(("groups", "expert"), None),
        P(("groups", "expert"), None),
        P(),
        P("expert", None, None),
        P("expert", None, None),
        P("expert", None, None),
    )
    return jax.shard_map(
        body, mesh=mesh, in_specs=placed, out_specs=P(("groups", "expert"), None), check_vma=False
    )
```

```python
import functools
import jax
import jax.numpy as jnp
from jax import lax
from jax.experimental import pallas as pl
from jax.experimental.pallas import tpu as pltpu
from jax.sharding import PartitionSpec as P

LANES = 128
STRIDE = 2
OFFSETS = {"first": 0, "relay": 1, "corner": 2, "expert": 3, "sum": 4, "second": 5, "home": 6}


def kernel(slabs, a_ref, wo_hbm, gain_ref, dense_ref, wg_hbm, wu_hbm, wd_hbm, out_ref, wo, w, wd,
           part, part_send, part_recv, t1_send, t1_recv, keep1, t2_send, t2_recv, keep2, t3_send,
           t3_recv, state, rows, hidden, y, y_send, y_recv, v1_send, v1_recv, v2_send, v2_recv,
           keep3, v3_send, v3_recv, load_sem, ps, pr, t1s, t1r, t2s, t2r, t3s, t3r, zs, zr, fs, fr,
           ds, dr, cs, cr, ys, yr, v1s, v1r, v2s, v2r, v3s, v3r):
    f32, bf16 = jnp.float32, jnp.bfloat16
    me = lax.axis_index("expert")
    q = me // 8
    yy = (me // 4) % 2
    xx = (me // 2) % 2
    cc = me % 2
    low = q % 2
    inner = me % 8
    core = me + 1 - 2 * cc
    xnbr = me + 2 - 4 * xx
    ynbr = me + 4 - 8 * yy
    znbr = me + 8 - 16 * low
    half = wo.shape[1] // 2
    units = wd.shape[0]
    rows_dev = out_ref.shape[0]
    first_nbr, second_nbr = (ynbr, xnbr), (xnbr, ynbr)
    second_at = (xx, yy)

    loads = [pltpu.make_async_copy(wo_hbm, wo, load_sem.at[0]),
             pltpu.make_async_copy(wg_hbm, w.at[:, 0:units], load_sem.at[1]),
             pltpu.make_async_copy(wu_hbm, w.at[:, units:2 * units], load_sem.at[2]),
             pltpu.make_async_copy(wd_hbm, wd, load_sem.at[3])]
    for load in loads:
        load.start()

    def slab_at(k):
        return lax.rem(q + k, slabs)

    barrier = pltpu.get_barrier_semaphore()
    others = [core, xnbr, ynbr] + [slab_at(k) * 8 + inner for k in range(1, slabs)]
    for other in others:
        pl.semaphore_signal(barrier, inc=1, device_id={"expert": other},
                            device_id_type=pl.DeviceIdType.MESH)

    sent = []

    def copy(src, dst, send_sem, recv_sem, device):
        return pltpu.make_async_remote_copy(
            src_ref=src, dst_ref=dst, send_sem=send_sem, recv_sem=recv_sem,
            device_id={"expert": device}, device_id_type=pl.DeviceIdType.MESH)

    def send(*args):
        made = copy(*args)
        made.start()
        sent.append(made)

    def wait(*args):
        copy(*args).wait_recv()

    loads[0].wait()
    chunk = min(512, half)
    heads = a_ref[...].reshape(16 * rows_dev, a_ref.shape[2])

    for h in range(2):
        @pl.loop(0, half // chunk)
        def _(j, h=h):
            at = pl.ds(pl.multiple_of(h * half + j * chunk, chunk), chunk)
            to = pl.ds(pl.multiple_of(j * chunk, chunk), chunk)
            r = jnp.dot(heads, wo[:, at], preferred_element_type=f32)
            r = r.reshape(2, 2, 2, 2, rows_dev, chunk)
            even, odd = r[:, :, :, 0], r[:, :, :, 1]
            part[h, :, :, :, :, to] = jnp.where(cc == 0, even, odd)
            part_send[h, :, :, :, :, to] = jnp.where(cc == 0, odd, even).astype(bf16)

        if h == 0:
            pl.semaphore_wait(barrier, len(others))
        send(part_send.at[h], part_recv.at[h], ps.at[h], pr.at[h], core)

    for h in range(2):
        wait(part_send.at[h], part_recv.at[h], ps.at[h], pr.at[h], core)
        if h == 0:
            away = part[0, :, 1 - yy] + part_recv[0, :, 1 - yy].astype(f32)
        else:
            away = part[1, :, :, 1 - xx] + part_recv[1, :, :, 1 - xx].astype(f32)
        t1_send[h] = away.astype(bf16)
        send(t1_send.at[h], t1_recv.at[h], t1s.at[h], t1r.at[h], first_nbr[h])
    keep1[0] = part[0, :, yy] + part_recv[0, :, yy].astype(f32)
    keep1[1] = part[1, :, :, xx] + part_recv[1, :, :, xx].astype(f32)
    for h in range(2):
        wait(t1_send.at[h], t1_recv.at[h], t1s.at[h], t1r.at[h], first_nbr[h])
        at = second_at[h]
        t2_send[h] = (keep1[h, :, 1 - at] + t1_recv[h, :, 1 - at].astype(f32)).astype(bf16)
        send(t2_send.at[h], t2_recv.at[h], t2s.at[h], t2r.at[h], second_nbr[h])
        keep2[h] = keep1[h, :, at] + t1_recv[h, :, at].astype(f32)
    for h in range(2):
        wait(t2_send.at[h], t2_recv.at[h], t2s.at[h], t2r.at[h], second_nbr[h])
        t3_send[h] = (keep2[h, 1 - low] + t2_recv[h, 1 - low].astype(f32)).astype(bf16)
        send(t3_send.at[h], t3_recv.at[h], t3s.at[h], t3r.at[h], znbr)
        state[h] = keep2[h, low] + t2_recv[h, low].astype(f32)
    square = 0.0
    for h in range(2):
        wait(t3_send.at[h], t3_recv.at[h], t3s.at[h], t3r.at[h], znbr)
        total = state[h] + t3_recv[h].astype(f32)
        state[h] = total
        square += jnp.sum(total * total, axis=-1, keepdims=True)
    scale = lax.rsqrt(square / (2 * half) + 1e-06)
    for h in range(2):
        gain = gain_ref[:, h * half:(h + 1) * half].astype(f32)
        rows[q, yy, xx, cc, h, :, 0:half] = (state[h] * scale * gain).astype(bf16)
        rows[q, yy, xx, cc, h, :, half:half + LANES] = dense_ref[h]

    own = rows.at[q, yy, xx, cc]
    for k in range(1, slabs):
        send(own, own, zs.at[k], zr.at[k], slab_at(k) * 8 + inner)

    def first(k):
        s = slab_at(slabs - k)
        block = rows.at[s, yy, xx, cc]
        if k:
            wait(block, block, zs.at[k], zr.at[k], slab_at(k) * 8 + inner)
        send(block, block, fs.at[k, 0], fr.at[k, 0], xnbr)
        send(block, block, fs.at[k, 1], fr.at[k, 1], ynbr)
        send(block, block, cs.at[k, 0], cr.at[k, 0], core)

    def relay(k):
        s = slab_at(slabs - k)
        block = rows.at[s, yy, 1 - xx, cc]
        wait(block, block, fs.at[k, 0], fr.at[k, 0], xnbr)
        send(block.at[0], block.at[0], ds.at[k, 0], dr.at[k, 0], ynbr)
        send(block, block, cs.at[k, 1], cr.at[k, 1], core)
        block = rows.at[s, 1 - yy, xx, cc]
        wait(block, block, fs.at[k, 1], fr.at[k, 1], ynbr)
        send(block.at[1], block.at[1], ds.at[k, 1], dr.at[k, 1], xnbr)
        send(block, block, cs.at[k, 2], cr.at[k, 2], core)

    def corner(k):
        s = slab_at(slabs - k)
        block = rows.at[s, 1 - yy, 1 - xx, cc]
        wait(block.at[0], block.at[0], ds.at[k, 0], dr.at[k, 0], ynbr)
        wait(block.at[1], block.at[1], ds.at[k, 1], dr.at[k, 1], xnbr)
        send(block, block, cs.at[k, 3], cr.at[k, 3], core)

    def expert(k):
        s = slab_at(slabs - k)
        for i, (ay, ax) in enumerate([(yy, xx), (yy, 1 - xx), (1 - yy, xx), (1 - yy, 1 - xx)]):
            block = rows.at[s, ay, ax, 1 - cc]
            wait(block, block, cs.at[k, i], cr.at[k, i], core)
        if k == 0:
            loads[1].wait()
            loads[2].wait()
        count = 8 * rows_dev
        wide = min(256, units)

        @pl.loop(0, 2 * units // wide)
        def _(n):
            at = pl.ds(pl.multiple_of(n * wide, wide), wide)
            total = jnp.dot(rows[s, :, :, :, 0, :, 0:half].reshape(count, half), w[0:half, at],
                            preferred_element_type=f32)
            total += jnp.dot(rows[s, :, :, :, 1, :, 0:half].reshape(count, half),
                             w[half:2 * half, at], preferred_element_type=f32)
            hidden[:, at] = total

        act = (jax.nn.silu(hidden[:, 0:units]) * hidden[:, units:2 * units]).astype(bf16)
        lane = lax.broadcasted_iota(jnp.int32, (count, LANES), 1)
        weight = (rows[s, :, :, :, 0, :, half:half + LANES].astype(f32)
                  + rows[s, :, :, :, 1, :, half:half + LANES].astype(f32)).reshape(count, LANES)
        weight = jnp.sum(jnp.where(lane == me // 2, weight, 0.0), axis=1, keepdims=True)
        if k == 0:
            loads[3].wait()
        for h in range(2):
            @pl.loop(0, half // chunk)
            def _(j, h=h):
                at = pl.ds(pl.multiple_of(h * half + j * chunk, chunk), chunk)
                to = pl.ds(pl.multiple_of(j * chunk, chunk), chunk)
                r = jnp.dot(act, wd[:, at], preferred_element_type=f32) * weight
                r = r.reshape(2, 2, 2, rows_dev, chunk)
                even, odd = r[:, :, 0], r[:, :, 1]
                y[k % y.shape[0], h, :, :, :, to] = jnp.where(cc == 0, even, odd)
                y_send[k, h, :, :, :, to] = jnp.where(cc == 0, odd, even).astype(bf16)
            send(y_send.at[k, h], y_recv.at[k, h], ys.at[k, h], yr.at[k, h], core)

    def sum_core(k):
        i = k % y.shape[0]
        for h in range(2):
            wait(y_send.at[k, h], y_recv.at[k, h], ys.at[k, h], yr.at[k, h], core)
            if h == 0:
                away = y[i, 0, 1 - yy] + y_recv[k, 0, 1 - yy].astype(f32)
            else:
                away = y[i, 1, :, 1 - xx] + y_recv[k, 1, :, 1 - xx].astype(f32)
            v1_send[k, h] = away.astype(bf16)
            send(v1_send.at[k, h], v1_recv.at[k, h], v1s.at[k, h], v1r.at[k, h], first_nbr[h])

    def second(k):
        i = k % y.shape[0]
        for h in range(2):
            wait(v1_send.at[k, h], v1_recv.at[k, h], v1s.at[k, h], v1r.at[k, h], first_nbr[h])
            at = second_at[h]

            def summed(b):
                mid = (yy, b) if h == 0 else (b, xx)
                return (y[i, h, mid[0], mid[1]] + y_recv[k, h, mid[0], mid[1]].astype(f32)
                        + v1_recv[k, h, b].astype(f32))
            v2_send[k, h] = summed(1 - at).astype(bf16)
            send(v2_send.at[k, h], v2_recv.at[k, h], v2s.at[k, h], v2r.at[k, h], second_nbr[h])
            keep3[k, h] = summed(at)

    def home(k):
        for h in range(2):
            wait(v2_send.at[k, h], v2_recv.at[k, h], v2s.at[k, h], v2r.at[k, h], second_nbr[h])
            total = keep3[k, h] + v2_recv[k, h].astype(f32)
            if k:
                v3_send[k, h] = total.astype(bf16)
            else:
                state[h] = state[h] + total
        if k:
            send(v3_send.at[k], v3_recv.at[k], v3s.at[k], v3r.at[k], slab_at(slabs - k) * 8 + inner)

    steps = {"first": first, "relay": relay, "corner": corner, "expert": expert, "sum": sum_core,
             "second": second, "home": home}
    order = sorted((k * STRIDE + OFFSETS[name], -OFFSETS[name], k, name)
                   for k in range(slabs) for name in steps)
    for _, _, k, name in order:
        steps[name](k)
    for k in range(1, slabs):
        wait(v3_send.at[k], v3_recv.at[k], v3s.at[k], v3r.at[k], slab_at(k) * 8 + inner)
    for h in range(2):
        total = state[h]
        for k in range(1, slabs):
            total = total + v3_recv[k, h].astype(f32)
        out_ref[:, h * half:(h + 1) * half] = total.astype(bf16)
    for made in sent:
        made.wait_send()


def body(attn_heads, out_proj, norm_gain, routes, gate_weights, expert_home, w_gate, w_up, w_down):
    width = out_proj.shape[2]
    rows_dev = routes.shape[0]
    units = w_down.shape[1]
    slabs = lax.axis_size("expert") // 8
    half = width // 2
    bf16, f32 = jnp.bfloat16, jnp.float32
    named = routes[:, :, None] == jnp.arange(expert_home.shape[0], dtype=jnp.int32)
    homes = jnp.sum(jnp.where(named, expert_home, 0), axis=2)
    at = homes[:, :, None] == jnp.arange(LANES, dtype=jnp.int32)
    dense = jnp.sum(jnp.where(at, gate_weights[:, :, None], 0.0), axis=1)
    coarse = lax.reduce_precision(dense, 8, 7)
    dense = jnp.stack([coarse, dense - coarse]).astype(bf16)
    heads = attn_heads[0].reshape(16, rows_dev, attn_heads.shape[2])
    vmem, dma = pltpu.VMEM, pltpu.SemaphoreType.DMA
    blk = (rows_dev, half)
    ring = min(slabs, 4)
    scratch = [
        vmem(out_proj.shape[1:], bf16), vmem((width, 2 * units), bf16), vmem((units, width), bf16),
        vmem((2, 2, 2, 2) + blk, f32), vmem((2, 2, 2, 2) + blk, bf16), vmem((2, 2, 2, 2) + blk, bf16),
        vmem((2, 2, 2) + blk, bf16), vmem((2, 2, 2) + blk, bf16), vmem((2, 2, 2) + blk, f32),
        vmem((2, 2) + blk, bf16), vmem((2, 2) + blk, bf16), vmem((2, 2) + blk, f32),
        vmem((2,) + blk, bf16), vmem((2,) + blk, bf16), vmem((2,) + blk, f32),
        vmem((slabs, 2, 2, 2, 2, rows_dev, half + LANES), bf16),
        vmem((8 * rows_dev, 2 * units), f32),
        vmem((ring, 2, 2, 2) + blk, f32),
        vmem((slabs, 2, 2, 2) + blk, bf16), vmem((slabs, 2, 2, 2) + blk, bf16),
        vmem((slabs, 2, 2) + blk, bf16), vmem((slabs, 2, 2) + blk, bf16),
        vmem((slabs, 2) + blk, bf16), vmem((slabs, 2) + blk, bf16),
        vmem((slabs, 2) + blk, f32),
        vmem((slabs, 2) + blk, bf16), vmem((slabs, 2) + blk, bf16),
        dma((4,)),
    ]
    for shape in [(2,)] * 4 + [(slabs,)] + [(slabs, 2)] * 2 + [(slabs, 4)] + [(slabs, 2)] * 3 + [(slabs,)]:
        scratch += [dma(shape), dma(shape)]
    inside = pl.BlockSpec(memory_space=pltpu.VMEM)
    outside = pl.BlockSpec(memory_space=pl.ANY)
    return pl.pallas_call(
        functools.partial(kernel, slabs),
        out_shape=jax.ShapeDtypeStruct((rows_dev, width), bf16),
        in_specs=[inside, outside, inside, inside, outside, outside, outside],
        out_specs=inside,
        scratch_shapes=scratch,
        compiler_params=pltpu.CompilerParams(
            collective_id=0, has_side_effects=True, vmem_limit_bytes=60 * 2**20
        ),
    )(heads, out_proj[0], norm_gain[None, :], dense, w_gate[0], w_up[0], w_down[0])


def solution(mesh):
    placed = (
        P(("groups", "expert"), None, None),
        P("expert", None, None),
        P(),
        P(("groups", "expert"), None),
        P(("groups", "expert"), None),
        P(),
        P("expert", None, None),
        P("expert", None, None),
        P("expert", None, None),
    )
    return jax.shard_map(
        body, mesh=mesh, in_specs=placed, out_specs=P(("groups", "expert"), None), check_vma=False
    )
```

```python
import functools
import jax
import jax.numpy as jnp
from jax import lax
from jax.experimental import pallas as pl
from jax.experimental.pallas import tpu as pltpu
from jax.sharding import PartitionSpec as P

LANES = 128
PLAN = {"first": (1, 0), "relay": (1, 1), "corner": (1, 2), "expert": (1, 3), "sum": (1, 4),
        "second": (1, 5), "home": (1, 6)}
PEERS = (7, 6, 5, 3, 4, 2, 1)


def flip(value, mask):
    for bit in range(mask.bit_length()):
        if mask >> bit & 1:
            value = value + (1 << bit) - (2 << bit) * ((value // (1 << bit)) % 2)
    return value


def kernel(slabs, home_ref, a_hbm, wo_hbm, gain_hbm, routes_hbm, gates_hbm, wg_hbm, wu_hbm, wd_hbm,
           out_ref, a_ref, gain_ref, routes_ref, gates_ref, wo, w, wd, part, part_send, part_recv,
           group_send, group_recv, state, rows, hidden, y, y_send, y_recv, v1_send, v1_recv,
           v2_send, v2_recv, keep3, v3_send, v3_recv, load_sem, ps, pr, gs, gr, zs, zr, fs, fr,
           ds, dr, cs, cr, ys, yr, v1s, v1r, v2s, v2r, v3s, v3r):
    f32, bf16 = jnp.float32, jnp.bfloat16
    me = lax.axis_index("expert")
    q = me // 8
    yy = (me // 4) % 2
    xx = (me // 2) % 2
    cc = me % 2
    low = q % 2
    inner = me % 8
    core = me + 1 - 2 * cc
    xnbr = me + 2 - 4 * xx
    ynbr = me + 4 - 8 * yy
    half = wo.shape[1] // 2
    units = wd.shape[0]
    rows_dev = out_ref.shape[0]
    first_nbr, second_nbr = (ynbr, xnbr), (xnbr, ynbr)
    second_at = (xx, yy)

    loads = [pltpu.make_async_copy(wo_hbm, wo, load_sem.at[0]),
             pltpu.make_async_copy(wg_hbm, w.at[:, 0:units], load_sem.at[1]),
             pltpu.make_async_copy(wu_hbm, w.at[:, units:2 * units], load_sem.at[2]),
             pltpu.make_async_copy(wd_hbm, wd, load_sem.at[3]),
             pltpu.make_async_copy(a_hbm, a_ref, load_sem.at[4]),
             pltpu.make_async_copy(gain_hbm, gain_ref, load_sem.at[5]),
             pltpu.make_async_copy(routes_hbm, routes_ref, load_sem.at[6]),
             pltpu.make_async_copy(gates_hbm, gates_ref, load_sem.at[7])]
    for i in (4, 0, 6, 7, 5, 1, 2, 3):
        loads[i].start()

    def slab_at(k):
        return flip(q, k)

    barrier = pltpu.get_barrier_semaphore()
    others = ([core] + [flip(me, 2 * i) for i in PEERS]
              + [slab_at(k) * 8 + inner for k in range(2, slabs)])
    for other in others:
        pl.semaphore_signal(barrier, inc=1, device_id={"expert": other},
                            device_id_type=pl.DeviceIdType.MESH)

    sent = []

    def copy(src, dst, send_sem, recv_sem, device):
        return pltpu.make_async_remote_copy(
            src_ref=src, dst_ref=dst, send_sem=send_sem, recv_sem=recv_sem,
            device_id={"expert": device}, device_id_type=pl.DeviceIdType.MESH)

    def send(*args):
        made = copy(*args)
        made.start()
        sent.append(made)

    def wait(*args):
        copy(*args).wait_recv()

    loads[6].wait()
    loads[7].wait()
    homes = jnp.zeros(routes_ref.shape, jnp.int32)
    for e in range(home_ref.shape[0]):
        homes = jnp.where(routes_ref[...] == e, home_ref[e], homes)
    at_pair = lax.broadcasted_iota(jnp.int32, (LANES, rows_dev), 0)
    dense = jnp.zeros((LANES, rows_dev), f32)
    for i in range(routes_ref.shape[0]):
        dense += jnp.where(homes[i:i + 1] == at_pair, gates_ref[i:i + 1, :], 0.0)
    dense = dense.T
    coarse = dense.astype(bf16)
    rows[q, yy, xx, cc, 0, :, half:half + LANES] = coarse
    rows[q, yy, xx, cc, 1, :, half:half + LANES] = (dense - coarse.astype(f32)).astype(bf16)
    loads[4].wait()
    loads[0].wait()
    chunk = min(512, half)
    heads = a_ref[...].reshape(16 * rows_dev, a_ref.shape[2])

    for h in range(2):
        @pl.loop(0, half // chunk)
        def _(j, h=h):
            at = pl.ds(pl.multiple_of(h * half + j * chunk, chunk), chunk)
            to = pl.ds(pl.multiple_of(j * chunk, chunk), chunk)
            r = jnp.dot(heads, wo[:, at], preferred_element_type=f32)
            r = r.reshape(2, 2, 2, 2, rows_dev, chunk)
            even, odd = r[:, :, :, 0], r[:, :, :, 1]
            part[h, :, :, :, :, to] = jnp.where(cc == 0, even, odd)
            part_send[h, :, :, :, :, to] = jnp.where(cc == 0, odd, even).astype(bf16)

        if h == 0:
            pl.semaphore_wait(barrier, len(others))
        send(part_send.at[h], part_recv.at[h], ps.at[h], pr.at[h], core)

    for h in range(2):
        wait(part_send.at[h], part_recv.at[h], ps.at[h], pr.at[h], core)
        for i, mask in enumerate(PEERS):
            at = (h, flip(low, mask >> 2), flip(yy, mask >> 1 & 1), flip(xx, mask & 1))
            group_send[h, i] = (part[at] + part_recv[at].astype(f32)).astype(bf16)
            send(group_send.at[h, i], group_recv.at[h, i], gs.at[h, i], gr.at[h, i], flip(me, 2 * mask))
        state[h] = part[h, low, yy, xx] + part_recv[h, low, yy, xx].astype(f32)
    square = 0.0
    for h in range(2):
        total = state[h]
        for i, mask in reversed(tuple(enumerate(PEERS))):
            wait(group_send.at[h, i], group_recv.at[h, i], gs.at[h, i], gr.at[h, i], flip(me, 2 * mask))
            total += group_recv[h, i].astype(f32)
        state[h] = total
        square += jnp.sum(total * total, axis=-1, keepdims=True)
    scale = lax.rsqrt(square / (2 * half) + 1e-06)
    loads[5].wait()
    gain = gain_ref[...].astype(f32)
    for i in range(2 * half // LANES):
        h, to = i * LANES // half, i * LANES % half
        rows[q, yy, xx, cc, h, :, to:to + LANES] = (
            state[h, :, to:to + LANES] * scale * gain[i:i + 1]).astype(bf16)

    own = rows.at[q, yy, xx, cc]
    for k in range(1, slabs):
        send(own, own, zs.at[k], zr.at[k], slab_at(k) * 8 + inner)

    def first(k):
        s = slab_at(k)
        block = rows.at[s, yy, xx, cc]
        if k:
            wait(block, block, zs.at[k], zr.at[k], slab_at(k) * 8 + inner)
        send(block, block, fs.at[k, 0], fr.at[k, 0], xnbr)
        send(block, block, fs.at[k, 1], fr.at[k, 1], ynbr)
        send(block, block, cs.at[k, 0], cr.at[k, 0], core)

    def relay(k):
        s = slab_at(k)
        block = rows.at[s, yy, 1 - xx, cc]
        wait(block, block, fs.at[k, 0], fr.at[k, 0], xnbr)
        send(block.at[0], block.at[0], ds.at[k, 0], dr.at[k, 0], ynbr)
        send(block, block, cs.at[k, 1], cr.at[k, 1], core)
        block = rows.at[s, 1 - yy, xx, cc]
        wait(block, block, fs.at[k, 1], fr.at[k, 1], ynbr)
        send(block.at[1], block.at[1], ds.at[k, 1], dr.at[k, 1], xnbr)
        send(block, block, cs.at[k, 2], cr.at[k, 2], core)

    def corner(k):
        s = slab_at(k)
        block = rows.at[s, 1 - yy, 1 - xx, cc]
        wait(block.at[0], block.at[0], ds.at[k, 0], dr.at[k, 0], ynbr)
        wait(block.at[1], block.at[1], ds.at[k, 1], dr.at[k, 1], xnbr)
        send(block, block, cs.at[k, 3], cr.at[k, 3], core)

    def expert(k):
        s = slab_at(k)
        for i, (ay, ax) in enumerate([(yy, xx), (yy, 1 - xx), (1 - yy, xx), (1 - yy, 1 - xx)]):
            block = rows.at[s, ay, ax, 1 - cc]
            wait(block, block, cs.at[k, i], cr.at[k, i], core)
        if k == 0:
            loads[1].wait()
            loads[2].wait()
        count = 8 * rows_dev
        wide = min(256, units)

        @pl.loop(0, 2 * units // wide)
        def _(n):
            at = pl.ds(pl.multiple_of(n * wide, wide), wide)
            total = jnp.dot(rows[s, :, :, :, 0, :, 0:half].reshape(count, half), w[0:half, at],
                            preferred_element_type=f32)
            total += jnp.dot(rows[s, :, :, :, 1, :, 0:half].reshape(count, half),
                             w[half:2 * half, at], preferred_element_type=f32)
            hidden[:, at] = total

        act = (jax.nn.silu(hidden[:, 0:units]) * hidden[:, units:2 * units]).astype(bf16)
        lane = lax.broadcasted_iota(jnp.int32, (count, LANES), 1)
        weight = (rows[s, :, :, :, 0, :, half:half + LANES].astype(f32)
                  + rows[s, :, :, :, 1, :, half:half + LANES].astype(f32)).reshape(count, LANES)
        weight = jnp.sum(jnp.where(lane == me // 2, weight, 0.0), axis=1, keepdims=True)
        if k == 0:
            loads[3].wait()
        for h in range(2):
            @pl.loop(0, half // chunk)
            def _(j, h=h):
                at = pl.ds(pl.multiple_of(h * half + j * chunk, chunk), chunk)
                to = pl.ds(pl.multiple_of(j * chunk, chunk), chunk)
                r = jnp.dot(act, wd[:, at], preferred_element_type=f32) * weight
                r = r.reshape(2, 2, 2, rows_dev, chunk)
                even, odd = r[:, :, 0], r[:, :, 1]
                y[k % y.shape[0], h, :, :, :, to] = jnp.where(cc == 0, even, odd)
                y_send[k, h, :, :, :, to] = jnp.where(cc == 0, odd, even).astype(bf16)
            send(y_send.at[k, h], y_recv.at[k, h], ys.at[k, h], yr.at[k, h], core)

    def sum_core(k):
        i = k % y.shape[0]
        for h in range(2):
            wait(y_send.at[k, h], y_recv.at[k, h], ys.at[k, h], yr.at[k, h], core)
            if h == 0:
                away = y[i, 0, 1 - yy] + y_recv[k, 0, 1 - yy].astype(f32)
            else:
                away = y[i, 1, :, 1 - xx] + y_recv[k, 1, :, 1 - xx].astype(f32)
            v1_send[k, h] = away.astype(bf16)
            send(v1_send.at[k, h], v1_recv.at[k, h], v1s.at[k, h], v1r.at[k, h], first_nbr[h])

    def second(k):
        i = k % y.shape[0]
        for h in range(2):
            wait(v1_send.at[k, h], v1_recv.at[k, h], v1s.at[k, h], v1r.at[k, h], first_nbr[h])
            at = second_at[h]

            def summed(b):
                mid = (yy, b) if h == 0 else (b, xx)
                return (y[i, h, mid[0], mid[1]] + y_recv[k, h, mid[0], mid[1]].astype(f32)
                        + v1_recv[k, h, b].astype(f32))
            v2_send[k, h] = summed(1 - at).astype(bf16)
            send(v2_send.at[k, h], v2_recv.at[k, h], v2s.at[k, h], v2r.at[k, h], second_nbr[h])
            keep3[k, h] = summed(at)

    def home(k):
        for h in range(2):
            wait(v2_send.at[k, h], v2_recv.at[k, h], v2s.at[k, h], v2r.at[k, h], second_nbr[h])
            total = keep3[k, h] + v2_recv[k, h].astype(f32)
            if k:
                v3_send[k, h] = total.astype(bf16)
            else:
                state[h] = state[h] + total
        if k:
            send(v3_send.at[k], v3_recv.at[k], v3s.at[k], v3r.at[k], slab_at(k) * 8 + inner)

    steps = {"first": first, "relay": relay, "corner": corner, "expert": expert, "sum": sum_core,
             "second": second, "home": home}
    order = sorted((k * PLAN[name][0] + PLAN[name][1], -PLAN[name][1], k, name)
                   for k in range(slabs) for name in steps)
    for _, _, k, name in order:
        steps[name](k)
    for k in range(1, slabs):
        wait(v3_send.at[k], v3_recv.at[k], v3s.at[k], v3r.at[k], slab_at(k) * 8 + inner)
    for h in range(2):
        total = state[h]
        for k in range(1, slabs):
            total = total + v3_recv[k, h].astype(f32)
        out_ref[:, h * half:(h + 1) * half] = total.astype(bf16)
    for made in sent:
        made.wait_send()


def body(attn_heads, out_proj, norm_gain, routes, gate_weights, expert_home, w_gate, w_up, w_down):
    width = out_proj.shape[2]
    rows_dev = routes.shape[0]
    units = w_down.shape[1]
    slabs = lax.axis_size("expert") // 8
    half = width // 2
    bf16, f32 = jnp.bfloat16, jnp.float32
    heads = attn_heads[0].reshape(16, rows_dev, attn_heads.shape[2])
    vmem, dma = pltpu.VMEM, pltpu.SemaphoreType.DMA
    blk = (rows_dev, half)
    ring = min(slabs, 4)
    scratch = [
        vmem(heads.shape, bf16), vmem((width // LANES, LANES), bf16), vmem(routes.shape[::-1], jnp.int32),
        vmem(routes.shape[::-1], f32),
        vmem(out_proj.shape[1:], bf16), vmem((width, 2 * units), bf16), vmem((units, width), bf16),
        vmem((2, 2, 2, 2) + blk, f32), vmem((2, 2, 2, 2) + blk, bf16), vmem((2, 2, 2, 2) + blk, bf16),
        vmem((2, 7) + blk, bf16), vmem((2, 7) + blk, bf16), vmem((2,) + blk, f32),
        vmem((slabs, 2, 2, 2, 2, rows_dev, half + LANES), bf16),
        vmem((8 * rows_dev, 2 * units), f32),
        vmem((ring, 2, 2, 2) + blk, f32),
        vmem((slabs, 2, 2, 2) + blk, bf16), vmem((slabs, 2, 2, 2) + blk, bf16),
        vmem((slabs, 2, 2) + blk, bf16), vmem((slabs, 2, 2) + blk, bf16),
        vmem((slabs, 2) + blk, bf16), vmem((slabs, 2) + blk, bf16),
        vmem((slabs, 2) + blk, f32),
        vmem((slabs, 2) + blk, bf16), vmem((slabs, 2) + blk, bf16),
        dma((8,)),
    ]
    for shape in [(2,), (2, 7), (slabs,)] + [(slabs, 2)] * 2 + [(slabs, 4)] + [(slabs, 2)] * 3 + [(slabs,)]:
        scratch += [dma(shape), dma(shape)]
    inside = pl.BlockSpec(memory_space=pltpu.VMEM)
    outside = pl.BlockSpec(memory_space=pl.ANY)
    return pl.pallas_call(
        functools.partial(kernel, slabs),
        out_shape=jax.ShapeDtypeStruct((rows_dev, width), bf16),
        in_specs=[pl.BlockSpec(memory_space=pltpu.SMEM)] + [outside] * 8,
        out_specs=inside,
        scratch_shapes=scratch,
        compiler_params=pltpu.CompilerParams(
            collective_id=0, has_side_effects=True, vmem_limit_bytes=60 * 2**20
        ),
    )(expert_home, heads, out_proj[0], norm_gain.reshape(width // LANES, LANES), routes.T,
      gate_weights.T, w_gate[0], w_up[0], w_down[0])


def solution(mesh):
    placed = (
        P(("groups", "expert"), None, None),
        P("expert", None, None),
        P(),
        P(("groups", "expert"), None),
        P(("groups", "expert"), None),
        P(),
        P("expert", None, None),
        P("expert", None, None),
        P("expert", None, None),
    )
    return jax.shard_map(
        body, mesh=mesh, in_specs=placed, out_specs=P(("groups", "expert"), None), check_vma=False
    )
```

```python
import functools
import jax
import jax.numpy as jnp
from jax import lax
from jax.experimental import pallas as pl
from jax.experimental.pallas import tpu as pltpu
from jax.sharding import PartitionSpec as P

LANES = 128
PLAN = {'first': (1, -0.5), 'relay': (1, 1), 'corner': (1, 2), 'expert': (1, 3), 'sum': (1, 4), 'second': (1, 5), 'home': (1, 6)}
GATHER_DIRECT = ()
SUM_DIRECT = ()
PEERS = (7, 6, 5, 3, 4, 2, 1)


def flip(value, mask):
    for bit in range(mask.bit_length()):
        if mask >> bit & 1:
            value = value + (1 << bit) - (2 << bit) * ((value // (1 << bit)) % 2)
    return value


def kernel(slabs, home_ref, a_hbm, wo_hbm, gain_hbm, routes_hbm, gates_hbm, wg_hbm, wu_hbm, wd_hbm,
           out_ref, a_ref, gain_ref, routes_ref, gates_ref, wo, w, wd, part, part_send, part_recv,
           group_send, group_recv, state, rows, hidden, y, y_send, y_recv, v1_send, v1_recv,
           v2_send, v2_recv, keep3, v3_send, v3_recv, load_sem, ps, pr, gs, gr, zs, zr, fs, fr,
           ds, dr, cs, cr, ys, yr, v1s, v1r, v2s, v2r, v3s, v3r):
    f32, bf16 = jnp.float32, jnp.bfloat16
    me = lax.axis_index("expert")
    q = me // 8
    yy = (me // 4) % 2
    xx = (me // 2) % 2
    cc = me % 2
    low = q % 2
    inner = me % 8
    core = me + 1 - 2 * cc
    xnbr = me + 2 - 4 * xx
    ynbr = me + 4 - 8 * yy
    half = wo.shape[1] // 2
    units = wd.shape[0]
    rows_dev = out_ref.shape[0]
    first_nbr, second_nbr = (ynbr, xnbr), (xnbr, ynbr)
    second_at = (xx, yy)

    loads = [pltpu.make_async_copy(wo_hbm, wo, load_sem.at[0]),
             pltpu.make_async_copy(wg_hbm, w.at[:, 0:units], load_sem.at[1]),
             pltpu.make_async_copy(wu_hbm, w.at[:, units:2 * units], load_sem.at[2]),
             pltpu.make_async_copy(wd_hbm, wd, load_sem.at[3]),
             pltpu.make_async_copy(a_hbm, a_ref, load_sem.at[4]),
             pltpu.make_async_copy(gain_hbm, gain_ref, load_sem.at[5]),
             pltpu.make_async_copy(routes_hbm, routes_ref, load_sem.at[6]),
             pltpu.make_async_copy(gates_hbm, gates_ref, load_sem.at[7])]
    for i in (4, 0, 6, 7, 5, 1, 2, 3):
        loads[i].start()

    def slab_at(k):
        return flip(q, k)

    barrier = pltpu.get_barrier_semaphore()
    others = ([core] + [flip(me, 2 * i) for i in PEERS]
              + [slab_at(k) * 8 + inner for k in range(2, slabs)])
    for other in others:
        pl.semaphore_signal(barrier, inc=1, device_id={"expert": other},
                            device_id_type=pl.DeviceIdType.MESH)

    sent = []

    def copy(src, dst, send_sem, recv_sem, device):
        return pltpu.make_async_remote_copy(
            src_ref=src, dst_ref=dst, send_sem=send_sem, recv_sem=recv_sem,
            device_id={"expert": device}, device_id_type=pl.DeviceIdType.MESH)

    def send(*args):
        made = copy(*args)
        made.start()
        sent.append(made)

    def wait(*args):
        copy(*args).wait_recv()

    loads[6].wait()
    loads[7].wait()
    homes = jnp.zeros(routes_ref.shape, jnp.int32)
    for e in range(home_ref.shape[0]):
        homes = jnp.where(routes_ref[...] == e, home_ref[e], homes)
    at_pair = lax.broadcasted_iota(jnp.int32, (LANES, rows_dev), 0)
    dense = jnp.zeros((LANES, rows_dev), f32)
    for i in range(routes_ref.shape[0]):
        dense += jnp.where(homes[i:i + 1] == at_pair, gates_ref[i:i + 1, :], 0.0)
    dense = dense.T
    coarse = dense.astype(bf16)
    rows[q, yy, xx, cc, 0, :, half:half + LANES] = coarse
    rows[q, yy, xx, cc, 1, :, half:half + LANES] = (dense - coarse.astype(f32)).astype(bf16)
    loads[4].wait()
    loads[0].wait()
    chunk = min(512, half)
    heads = a_ref[...].reshape(16 * rows_dev, a_ref.shape[2])

    for h in range(2):
        @pl.loop(0, half // chunk)
        def _(j, h=h):
            at = pl.ds(pl.multiple_of(h * half + j * chunk, chunk), chunk)
            to = pl.ds(pl.multiple_of(j * chunk, chunk), chunk)
            r = jnp.dot(heads, wo[:, at], preferred_element_type=f32)
            r = r.reshape(2, 2, 2, 2, rows_dev, chunk)
            even, odd = r[:, :, :, 0], r[:, :, :, 1]
            part[h, :, :, :, :, to] = jnp.where(cc == 0, even, odd)
            part_send[h, :, :, :, :, to] = jnp.where(cc == 0, odd, even).astype(bf16)

        if h == 0:
            pl.semaphore_wait(barrier, len(others))
        send(part_send.at[h], part_recv.at[h], ps.at[h], pr.at[h], core)

    for h in range(2):
        wait(part_send.at[h], part_recv.at[h], ps.at[h], pr.at[h], core)
        for i, mask in enumerate(PEERS):
            at = (h, flip(low, mask >> 2), flip(yy, mask >> 1 & 1), flip(xx, mask & 1))
            group_send[h, i] = (part[at] + part_recv[at].astype(f32)).astype(bf16)
            send(group_send.at[h, i], group_recv.at[h, i], gs.at[h, i], gr.at[h, i], flip(me, 2 * mask))
        state[h] = part[h, low, yy, xx] + part_recv[h, low, yy, xx].astype(f32)
    square = 0.0
    for h in range(2):
        total = state[h]
        for i, mask in reversed(tuple(enumerate(PEERS))):
            wait(group_send.at[h, i], group_recv.at[h, i], gs.at[h, i], gr.at[h, i], flip(me, 2 * mask))
            total += group_recv[h, i].astype(f32)
        state[h] = total
        square += jnp.sum(total * total, axis=-1, keepdims=True)
    scale = lax.rsqrt(square / (2 * half) + 1e-06)
    loads[5].wait()
    gain = gain_ref[...].astype(f32)
    for i in range(2 * half // LANES):
        h, to = i * LANES // half, i * LANES % half
        rows[q, yy, xx, cc, h, :, to:to + LANES] = (
            state[h, :, to:to + LANES] * scale * gain[i:i + 1]).astype(bf16)

    def first(k):
        s = slab_at(k)
        block = rows.at[s, yy, xx, cc]
        if k:
            wait(block, block, zs.at[k], zr.at[k], slab_at(k) * 8 + inner)
        bit = 1
        while bit < (k & -k if k else slabs):
            send(block, block, zs.at[k + bit], zr.at[k + bit], slab_at(bit) * 8 + inner)
            bit *= 2
        send(block, block, fs.at[k, 0], fr.at[k, 0], xnbr)
        send(block, block, fs.at[k, 1], fr.at[k, 1], ynbr)
        if k in GATHER_DIRECT:
            send(block, block, ds.at[k, 0], dr.at[k, 0], flip(me, 6))
        send(block, block, cs.at[k, 0], cr.at[k, 0], core)

    def relay(k):
        s = slab_at(k)
        block = rows.at[s, yy, 1 - xx, cc]
        wait(block, block, fs.at[k, 0], fr.at[k, 0], xnbr)
        if k not in GATHER_DIRECT:
            send(block.at[0], block.at[0], ds.at[k, 0], dr.at[k, 0], ynbr)
        send(block, block, cs.at[k, 1], cr.at[k, 1], core)
        block = rows.at[s, 1 - yy, xx, cc]
        wait(block, block, fs.at[k, 1], fr.at[k, 1], ynbr)
        if k not in GATHER_DIRECT:
            send(block.at[1], block.at[1], ds.at[k, 1], dr.at[k, 1], xnbr)
        send(block, block, cs.at[k, 2], cr.at[k, 2], core)

    def corner(k):
        s = slab_at(k)
        block = rows.at[s, 1 - yy, 1 - xx, cc]
        if k in GATHER_DIRECT:
            wait(block, block, ds.at[k, 0], dr.at[k, 0], flip(me, 6))
        else:
            wait(block.at[0], block.at[0], ds.at[k, 0], dr.at[k, 0], ynbr)
            wait(block.at[1], block.at[1], ds.at[k, 1], dr.at[k, 1], xnbr)
        send(block, block, cs.at[k, 3], cr.at[k, 3], core)

    def expert(k):
        s = slab_at(k)
        for i, (ay, ax) in enumerate([(yy, xx), (yy, 1 - xx), (1 - yy, xx), (1 - yy, 1 - xx)]):
            block = rows.at[s, ay, ax, 1 - cc]
            wait(block, block, cs.at[k, i], cr.at[k, i], core)
        if k == 0:
            loads[1].wait()
            loads[2].wait()
        count = 8 * rows_dev
        wide = min(256, units)

        @pl.loop(0, 2 * units // wide)
        def _(n):
            at = pl.ds(pl.multiple_of(n * wide, wide), wide)
            total = jnp.dot(rows[s, :, :, :, 0, :, 0:half].reshape(count, half), w[0:half, at],
                            preferred_element_type=f32)
            total += jnp.dot(rows[s, :, :, :, 1, :, 0:half].reshape(count, half),
                             w[half:2 * half, at], preferred_element_type=f32)
            hidden[:, at] = total

        act = (jax.nn.silu(hidden[:, 0:units]) * hidden[:, units:2 * units]).astype(bf16)
        lane = lax.broadcasted_iota(jnp.int32, (count, LANES), 1)
        weight = (rows[s, :, :, :, 0, :, half:half + LANES].astype(f32)
                  + rows[s, :, :, :, 1, :, half:half + LANES].astype(f32)).reshape(count, LANES)
        weight = jnp.sum(jnp.where(lane == me // 2, weight, 0.0), axis=1, keepdims=True)
        if k == 0:
            loads[3].wait()
        for h in range(2):
            @pl.loop(0, half // chunk)
            def _(j, h=h):
                at = pl.ds(pl.multiple_of(h * half + j * chunk, chunk), chunk)
                to = pl.ds(pl.multiple_of(j * chunk, chunk), chunk)
                r = jnp.dot(act, wd[:, at], preferred_element_type=f32) * weight
                r = r.reshape(2, 2, 2, rows_dev, chunk)
                even, odd = r[:, :, 0], r[:, :, 1]
                y[k % y.shape[0], h, :, :, :, to] = jnp.where(cc == 0, even, odd)
                y_send[k, h, :, :, :, to] = jnp.where(cc == 0, odd, even).astype(bf16)
            send(y_send.at[k, h], y_recv.at[k, h], ys.at[k, h], yr.at[k, h], core)

    def straight(k):
        return ((v1_send.at[k, 0], v1_recv.at[k, 0], v1s.at[k, 0], v1r.at[k, 0], xnbr),
                (v1_send.at[k, 1], v1_recv.at[k, 1], v1s.at[k, 1], v1r.at[k, 1], ynbr),
                (v2_send.at[k], v2_recv.at[k], v2s.at[k, 0], v2r.at[k, 0], flip(me, 6)))

    def sum_core(k):
        i = k % y.shape[0]
        if k in SUM_DIRECT:
            for h in range(2):
                wait(y_send.at[k, h], y_recv.at[k, h], ys.at[k, h], yr.at[k, h], core)

            def summed(h, ay, ax):
                return (y[i, h, ay, ax] + y_recv[k, h, ay, ax].astype(f32)).astype(bf16)
            hops = straight(k)
            for h in range(2):
                v2_send[k, h] = summed(h, 1 - yy, 1 - xx)
            send(*hops[2])
            for h in range(2):
                v1_send[k, 0, h] = summed(h, yy, 1 - xx)
            send(*hops[0])
            for h in range(2):
                v1_send[k, 1, h] = summed(h, 1 - yy, xx)
            send(*hops[1])
            for h in range(2):
                keep3[k, h] = y[i, h, yy, xx] + y_recv[k, h, yy, xx].astype(f32)
            return
        for h in range(2):
            wait(y_send.at[k, h], y_recv.at[k, h], ys.at[k, h], yr.at[k, h], core)
            if h == 0:
                away = y[i, 0, 1 - yy] + y_recv[k, 0, 1 - yy].astype(f32)
            else:
                away = y[i, 1, :, 1 - xx] + y_recv[k, 1, :, 1 - xx].astype(f32)
            v1_send[k, h] = away.astype(bf16)
            send(v1_send.at[k, h], v1_recv.at[k, h], v1s.at[k, h], v1r.at[k, h], first_nbr[h])

    def second(k):
        i = k % y.shape[0]
        if k in SUM_DIRECT:
            return
        for h in range(2):
            wait(v1_send.at[k, h], v1_recv.at[k, h], v1s.at[k, h], v1r.at[k, h], first_nbr[h])
            at = second_at[h]

            def summed(b):
                mid = (yy, b) if h == 0 else (b, xx)
                return (y[i, h, mid[0], mid[1]] + y_recv[k, h, mid[0], mid[1]].astype(f32)
                        + v1_recv[k, h, b].astype(f32))
            v2_send[k, h] = summed(1 - at).astype(bf16)
            send(v2_send.at[k, h], v2_recv.at[k, h], v2s.at[k, h], v2r.at[k, h], second_nbr[h])
            keep3[k, h] = summed(at)

    def home(k):
        if k in SUM_DIRECT:
            for hop in straight(k):
                wait(*hop)
        for h in range(2):
            if k in SUM_DIRECT:
                total = (keep3[k, h] + v2_recv[k, h].astype(f32) + v1_recv[k, 0, h].astype(f32)
                         + v1_recv[k, 1, h].astype(f32))
            else:
                wait(v2_send.at[k, h], v2_recv.at[k, h], v2s.at[k, h], v2r.at[k, h], second_nbr[h])
                total = keep3[k, h] + v2_recv[k, h].astype(f32)
            if k:
                v3_send[k, h] = total.astype(bf16)
            else:
                state[h] = state[h] + total
        if k:
            send(v3_send.at[k], v3_recv.at[k], v3s.at[k], v3r.at[k], slab_at(k) * 8 + inner)

    steps = {"first": first, "relay": relay, "corner": corner, "expert": expert, "sum": sum_core,
             "second": second, "home": home}
    order = sorted((k * PLAN[name][0] + PLAN[name][1], -PLAN[name][1], k, name)
                   for k in range(slabs) for name in steps)
    for _, _, k, name in order:
        steps[name](k)
    for k in range(1, slabs):
        wait(v3_send.at[k], v3_recv.at[k], v3s.at[k], v3r.at[k], slab_at(k) * 8 + inner)
    for h in range(2):
        total = state[h]
        for k in range(1, slabs):
            total = total + v3_recv[k, h].astype(f32)
        out_ref[:, h * half:(h + 1) * half] = total.astype(bf16)
    for made in sent:
        made.wait_send()


def body(attn_heads, out_proj, norm_gain, routes, gate_weights, expert_home, w_gate, w_up, w_down):
    width = out_proj.shape[2]
    rows_dev = routes.shape[0]
    units = w_down.shape[1]
    slabs = lax.axis_size("expert") // 8
    half = width // 2
    bf16, f32 = jnp.bfloat16, jnp.float32
    heads = attn_heads[0].reshape(16, rows_dev, attn_heads.shape[2])
    vmem, dma = pltpu.VMEM, pltpu.SemaphoreType.DMA
    blk = (rows_dev, half)
    ring = min(slabs, 4)
    scratch = [
        vmem(heads.shape, bf16), vmem((width // LANES, LANES), bf16), vmem(routes.shape[::-1], jnp.int32),
        vmem(routes.shape[::-1], f32),
        vmem(out_proj.shape[1:], bf16), vmem((width, 2 * units), bf16), vmem((units, width), bf16),
        vmem((2, 2, 2, 2) + blk, f32), vmem((2, 2, 2, 2) + blk, bf16), vmem((2, 2, 2, 2) + blk, bf16),
        vmem((2, 7) + blk, bf16), vmem((2, 7) + blk, bf16), vmem((2,) + blk, f32),
        vmem((slabs, 2, 2, 2, 2, rows_dev, half + LANES), bf16),
        vmem((8 * rows_dev, 2 * units), f32),
        vmem((ring, 2, 2, 2) + blk, f32),
        vmem((slabs, 2, 2, 2) + blk, bf16), vmem((slabs, 2, 2, 2) + blk, bf16),
        vmem((slabs, 2, 2) + blk, bf16), vmem((slabs, 2, 2) + blk, bf16),
        vmem((slabs, 2) + blk, bf16), vmem((slabs, 2) + blk, bf16),
        vmem((slabs, 2) + blk, f32),
        vmem((slabs, 2) + blk, bf16), vmem((slabs, 2) + blk, bf16),
        dma((8,)),
    ]
    for shape in [(2,), (2, 7), (slabs,)] + [(slabs, 2)] * 2 + [(slabs, 4)] + [(slabs, 2)] * 3 + [(slabs,)]:
        scratch += [dma(shape), dma(shape)]
    inside = pl.BlockSpec(memory_space=pltpu.VMEM)
    outside = pl.BlockSpec(memory_space=pl.ANY)
    return pl.pallas_call(
        functools.partial(kernel, slabs),
        out_shape=jax.ShapeDtypeStruct((rows_dev, width), bf16),
        in_specs=[pl.BlockSpec(memory_space=pltpu.SMEM)] + [outside] * 8,
        out_specs=inside,
        scratch_shapes=scratch,
        compiler_params=pltpu.CompilerParams(
            collective_id=0, has_side_effects=True, vmem_limit_bytes=60 * 2**20
        ),
    )(expert_home, heads, out_proj[0], norm_gain.reshape(width // LANES, LANES), routes.T,
      gate_weights.T, w_gate[0], w_up[0], w_down[0])


def solution(mesh):
    placed = (
        P(("groups", "expert"), None, None),
        P("expert", None, None),
        P(),
        P(("groups", "expert"), None),
        P(("groups", "expert"), None),
        P(),
        P("expert", None, None),
        P("expert", None, None),
        P("expert", None, None),
    )
    return jax.shard_map(
        body, mesh=mesh, in_specs=placed, out_specs=P(("groups", "expert"), None), check_vma=False
    )
```
